32 devices in a mesh: grp: 2 (over y), seq: 4 (over z), tp: 4 (over x, core).
Axes of the slice: x: 2, y: 2, z: 4, core: 2. Of those that a mesh axis runs over, the one named last changes fastest.
Arguments:
- grad_res: bfloat16 [4096, 4096], P(('grp', 'seq', 'tp')), parts along dimension 0, may hold values from -6 to 6
- features: bfloat16 [1536, 4608], P(('grp', 'seq', 'tp')), parts along dimension 0, may hold values from -70 to 70
- norm_gain: float32 [4608], replicated, may hold values from 0.1 to 1.9
- hidden_proj: bfloat16 [4608, 4608], P(None, 'tp'), may hold values from -0.09375 to 0.09375
- output_proj: bfloat16 [4608, 4096], P('tp'), may hold values from -0.09375 to 0.09375
- item_start: int32 [8, 32], P('grp'), parts along dimension 0, may hold values from 0 to 511, as said below
- item_len: int32 [8, 32], P('grp'), parts along dimension 0, may hold values from 3 to 6, as said below
- item_owner: int32 [8, 32], P('grp'), parts along dimension 0, may hold values from 0 to 3, as said below
Outputs:
- feat_grad: bfloat16 [1536, 4608], P(('grp', 'seq', 'tp')), parts along dimension 0
- grad_hidden: float32 [9216, 4608], P(('grp', 'seq'), 'tp'), parts along dimension 0
- grad_output: float32 [8192, 4608], P(('grp', 'seq'), 'tp'), parts along dimension 0
The draws below stay inside these ranges and needn't reach their ends.
There are 2 independent parts, one for each index of `grp`. The reference program is written for one: setup_inputs(seed, part) draws one part's arguments, and reference() takes and returns one part's arrays. A program takes and returns all parts, laid end to end along the dimension named above; an argument that names none is the same for every part. Nothing has to cross between parts.
Inputs may be any that keep to these rules, and one draw needn't show every extreme that they name: `item_start`: items of a shard do not share tokens and stand in increasing order; item i lies within tokens t * 128 to (t + 1) * 128 - 1 of its shard, t = i // 8. `item_owner`: for each tp index t there is a permutation P_t of the owners such that item i of shard s goes to P_t[(s + i % 8) % 4], t = i // 8; so every owner gets exactly 8 items of each tp index. `item_len`: the items of one owner and one tp index hold at most 48 tokens, and the items of one device that go to one owner at most 12; in every draw one owner reaches both.
All inputs are finite; a program needn't handle non-finite values.
Results may differ from the reference program's by a relative error of at most 0.013.
Values may be sent and summed in bfloat16 or wider, within the bound.
A program may use at most 128 MiB of HBM per device.

```python
import math
import jax
import jax.numpy as jnp
from jax import lax

D = 4096
M = 4608
TOK_DEV = 128
IMG_LANE = 8
LMAX = 6
TOK_SH = 512
TOKENS = 2048
BLK = 48
OWN_CAP = 192
OWN_ROWS = 768
N_SEQ = 4
N_TP = 4


def shuffled(lane_key):
    return jax.random.permutation(lane_key, N_SEQ)


def item_tables(key):
    subkeys = jax.random.split(key, 4)
    orders = jax.vmap(shuffled)(jax.random.split(subkeys[0], N_TP))
    shard_ids = jnp.arange(N_SEQ, dtype=jnp.int32)[:, None, None]
    lane_ids = jnp.arange(N_TP, dtype=jnp.int32)[None, :, None]
    slot_ids = jnp.arange(IMG_LANE, dtype=jnp.int32)[None, None, :]
    position = (shard_ids + slot_ids) % N_SEQ
    owners = orders[lane_ids, position].astype(jnp.int32)
    busiest = jax.random.randint(subkeys[1], (), 0, N_SEQ)
    short_len = jax.random.randint(subkeys[2], (N_SEQ, N_TP, IMG_LANE), LMAX // 2, LMAX + 1)
    lengths = jnp.where(owners == busiest, LMAX, short_len).astype(jnp.int32)
    spare_rows = TOK_DEV - jnp.sum(lengths, axis=2, keepdims=True)
    gap_rows = jax.random.randint(subkeys[3], (N_SEQ, N_TP, IMG_LANE), 0, spare_rows // (IMG_LANE + 1) + 1)
    end_rows = jnp.cumsum(gap_rows + lengths, axis=2)
    starts = (end_rows - lengths + lane_ids * TOK_DEV).astype(jnp.int32)
    table_shape = (N_SEQ, N_TP * IMG_LANE)
    return (starts.reshape(table_shape), lengths.reshape(table_shape), owners.reshape(table_shape))


def draw_item_start(key, part):
    tables = item_tables(key)
    return tables[0]


def draw_item_len(key, part):
    tables = item_tables(key)
    return tables[1]


def draw_item_owner(key, part):
    tables = item_tables(key)
    return tables[2]


def draw_features(key, part):
    key = jax.random.fold_in(key, 7)
    subkeys = jax.random.split(key, 4)
    log_ten = math.log(10.0)
    column_scale = jnp.exp(jax.random.uniform(subkeys[1], (1, M), minval=-0.5 * log_ten, maxval=0.5 * log_ten))
    offset = 2.0 * jax.random.truncated_normal(subkeys[2], -3.0, 3.0, (OWN_ROWS, 1))
    row_scale = jnp.exp(jax.random.uniform(subkeys[0], (OWN_ROWS, 1), minval=-0.5 * log_ten, maxval=0.5 * log_ten))
    base_values = jax.random.truncated_normal(subkeys[3], -4.0, 4.0, (OWN_ROWS, M))
    return (base_values * row_scale * column_scale + offset).astype(jnp.bfloat16)


def steps_of(key, shape, pieces, smallest, top_value):
    def one(axis_at, parts):
        draws = jax.random.uniform(jax.random.fold_in(jax.random.fold_in(key, 6), axis_at), (parts,), jnp.float32, smallest / len(pieces), top_value / len(pieces))
        return jnp.repeat(jnp.exp(draws), shape[axis_at] // parts).reshape((-1,) + (1,) * (len(shape) - axis_at - 1))

    level = one(*pieces[0])
    for cut in pieces[1:]:
        level = level * one(*cut)
    return level


def normal_values(stream_key, extent, scale, limit, cuts=(), held_as=jnp.bfloat16):
    factor_of = steps_of(stream_key, extent, cuts, -0.22, 0.18) if cuts else 1.0
    drawn = jax.random.normal(stream_key, extent, jnp.float32) * scale * factor_of
    return jnp.minimum(jnp.maximum(drawn, -limit), limit).astype(held_as)


def setup_inputs(seed: int = 0, part: int = 0) -> dict:
    splits = jax.random.split(jax.random.key(seed), 9)
    part_splits = jax.random.split(jax.random.fold_in(splits[8], part), 9)
    grad_res = normal_values(part_splits[0], (TOKENS, D), 1.0, 6.0, ((0, 16),))
    features = draw_features(jax.random.fold_in(jax.random.fold_in(splits[8], part), 71), part)
    norm_gain = jnp.clip(1.0 + 0.18 * jax.random.normal(splits[2], (M,), jnp.float32), 0.1, 1.9)
    hidden_proj = normal_values(splits[3], (M, M), M ** -0.5, 0.09375, ((1, 4),))
    output_proj = normal_values(splits[4], (M, D), M ** -0.5, 0.09375, ((0, 4),))
    item_start = draw_item_start(jax.random.fold_in(jax.random.fold_in(splits[8], part), 71), part)
    item_len = draw_item_len(jax.random.fold_in(jax.random.fold_in(splits[8], part), 71), part)
    item_owner = draw_item_owner(jax.random.fold_in(jax.random.fold_in(splits[8], part), 71), part)
    return dict(grad_res=grad_res, features=features, norm_gain=norm_gain, hidden_proj=hidden_proj, output_proj=output_proj, item_start=item_start, item_len=item_len, item_owner=item_owner)


EPSILON = 1e-06

def gelu_slope(pre_act):
    normal_cdf = 0.5 * (1.0 + lax.erf(pre_act * 0.7071067811865476))
    density = jnp.exp(-0.5 * pre_act * pre_act) * 0.3989422804014327
    return normal_cdf + pre_act * density

def routed_index(item_start, item_len, item_owner):
    starts = jnp.transpose(item_start.reshape(N_SEQ, N_TP, IMG_LANE), (1, 0, 2)).reshape(N_TP, N_SEQ * IMG_LANE)
    lengths = jnp.transpose(item_len.reshape(N_SEQ, N_TP, IMG_LANE), (1, 0, 2)).reshape(N_TP, N_SEQ * IMG_LANE)
    owners = jnp.transpose(item_owner.reshape(N_SEQ, N_TP, IMG_LANE), (1, 0, 2)).reshape(N_TP, N_SEQ * IMG_LANE)
    shard_row = jnp.arange(N_SEQ * IMG_LANE, dtype=jnp.int32) // IMG_LANE * TOK_SH
    owner_ids = jnp.arange(N_SEQ, dtype=jnp.int32)
    one_hot = owners[:, :, None] == owner_ids[None, None, :]
    sized_len = jnp.where(one_hot, lengths[:, :, None], 0)
    offsets = jnp.cumsum(sized_len, axis=1) - sized_len
    own_offset = lax.optimization_barrier(jnp.sum(jnp.where(one_hot, offsets, 0), axis=2)).astype(jnp.int32)
    place_index = jnp.arange(BLK, dtype=jnp.int32)[None, None, :, None]
    offset_wide = own_offset[None, :, None, :]
    matched = (owners[None, :, None, :] == owner_ids[:, None, None, None]) & (place_index >= offset_wide) & (place_index < offset_wide + lengths[None, :, None, :])
    token_row = shard_row[None, None, None, :] + starts[None, :, None, :] + place_index - offset_wide
    source_row = lax.optimization_barrier(jnp.sum(jnp.where(matched, token_row, 0), axis=3)).reshape(-1).astype(jnp.int32)
    present = jnp.any(matched, axis=3).reshape(-1)
    return (source_row, present)

def reference(grad_res, features, norm_gain, hidden_proj, output_proj, item_start, item_len, item_owner):
    source_row, present = routed_index(item_start, item_len, item_owner)
    picked = jnp.take(grad_res, source_row, axis=0)
    routed = jnp.where(present[:, None], picked, jnp.zeros((), grad_res.dtype))
    values = features.astype(jnp.float32)
    row_mean = lax.optimization_barrier(jnp.mean(values, axis=1, keepdims=True))
    centered = values - row_mean
    variance = lax.optimization_barrier(jnp.mean(centered * centered, axis=1, keepdims=True))
    inv_std = lax.rsqrt(variance + EPSILON)
    unit_rows = centered * inv_std
    normed = (unit_rows * norm_gain).astype(jnp.bfloat16)
    pre_act = jnp.dot(normed, hidden_proj, preferred_element_type=jnp.float32)
    activated = jax.nn.gelu(pre_act, approximate=False).astype(jnp.bfloat16)
    grad_act = jnp.dot(routed, output_proj.T, preferred_element_type=jnp.float32)
    grad_pre = (grad_act * gelu_slope(pre_act)).astype(jnp.bfloat16)
    grad_normed = jnp.dot(grad_pre, hidden_proj.T, preferred_element_type=jnp.float32)
    scaled = grad_normed * norm_gain
    grad_mean = lax.optimization_barrier(jnp.mean(scaled, axis=1, keepdims=True))
    cross_mean = lax.optimization_barrier(jnp.mean(scaled * unit_rows, axis=1, keepdims=True))
    feat_grad = ((scaled - grad_mean - unit_rows * cross_mean) * inv_std).astype(jnp.bfloat16)

    def owner_sum(totals, owner_id):
        first_row = owner_id * OWN_CAP
        normed_part = lax.dynamic_slice_in_dim(normed, first_row, OWN_CAP, 0)
        grad_part = lax.dynamic_slice_in_dim(grad_pre, first_row, OWN_CAP, 0)
        routed_part = lax.dynamic_slice_in_dim(routed, first_row, OWN_CAP, 0)
        active_part = lax.dynamic_slice_in_dim(activated, first_row, OWN_CAP, 0)
        hidden_term = jnp.dot(normed_part.T, grad_part, preferred_element_type=jnp.float32).astype(jnp.bfloat16)
        output_term = jnp.dot(routed_part.T, active_part, preferred_element_type=jnp.float32).astype(jnp.bfloat16)
        hidden_term = lax.optimization_barrier(hidden_term)
        output_term = lax.optimization_barrier(output_term)
        return ((totals[0] + hidden_term.astype(jnp.float32), totals[1] + output_term.astype(jnp.float32)), None)
    start_totals = (jnp.zeros((M, M), jnp.float32), jnp.zeros((D, M), jnp.float32))
    totals, ignored = lax.scan(owner_sum, start_totals, jnp.arange(N_SEQ, dtype=jnp.int32))
    return (feat_grad, totals[0] / N_SEQ, totals[1] / N_SEQ)
```

```python
import jax
import jax.numpy as jnp
from jax import lax
from jax.sharding import PartitionSpec as P

EPSILON = 1e-06


def gelu_slope(pre_act):
    normal_cdf = 0.5 * (1.0 + lax.erf(pre_act * 0.7071067811865476))
    density = jnp.exp(-0.5 * pre_act * pre_act) * 0.3989422804014327
    return normal_cdf + pre_act * density


def outgoing_rows(grad_res, starts, lengths, owners, base_row, seq_count, slot_rows):
    item_count = owners.shape[0]
    order_index = jnp.arange(item_count)
    same_owner = owners[:, None] == owners[None, :]
    earlier = order_index[None, :] < order_index[:, None]
    offset = jnp.sum(jnp.where(same_owner & earlier, lengths[None, :], 0), axis=1)
    destination = jnp.arange(seq_count)[:, None, None]
    place_index = jnp.arange(slot_rows)[None, :, None]
    matched = (
        (owners[None, None, :] == destination)
        & (place_index >= offset)
        & (place_index < offset + lengths)
    )
    local_row = starts - base_row + place_index - offset
    source_row = jnp.sum(jnp.where(matched, local_row, 0), axis=2).reshape(-1)
    filled = jnp.any(matched, axis=2).reshape(-1, 1)
    picked = jnp.take(grad_res, source_row, axis=0)
    picked = jnp.where(filled, picked, jnp.zeros((), picked.dtype))
    return picked.reshape(seq_count, slot_rows, grad_res.shape[1])


def compact_rows(incoming, owner_table, length_table, seq_index, own_rows):
    seq_count, slot_rows, model_width = incoming.shape
    counts = jnp.sum(jnp.where(owner_table == seq_index, length_table, 0), axis=1)
    starts_at = jnp.cumsum(counts) - counts
    position = jnp.arange(own_rows)[:, None]
    inside = (position >= starts_at[None, :]) & (position < (starts_at + counts)[None, :])
    flat_index = jnp.arange(seq_count)[None, :] * slot_rows + position - starts_at[None, :]
    slot_index = jnp.sum(jnp.where(inside, flat_index, 0), axis=1)
    present = jnp.any(inside, axis=1)[:, None]
    gathered = jnp.take(incoming.reshape(seq_count * slot_rows, model_width), slot_index, axis=0)
    return jnp.where(present, gathered, jnp.zeros((), gathered.dtype))


def per_device(
    grad_res, features, norm_gain, hidden_proj, output_proj, item_start, item_len, item_owner
):
    seq_count = lax.axis_size("seq")
    lane_count = lax.axis_size("tp")
    seq_index = lax.axis_index("seq")
    lane_index = lax.axis_index("tp")
    tok_rows = grad_res.shape[0]
    own_rows = features.shape[0]
    item_count = item_len.shape[1] // lane_count
    longest = own_rows // item_count
    slot_rows = longest * max(1, item_count // seq_count)
    values = features.astype(jnp.float32)
    row_mean = jnp.mean(values, axis=1, keepdims=True)
    centered = values - row_mean
    variance = jnp.mean(centered * centered, axis=1, keepdims=True)
    inv_std = lax.rsqrt(variance + EPSILON)
    unit_rows = centered * inv_std
    normed_own = (unit_rows * norm_gain).astype(jnp.bfloat16)
    normed = lax.all_gather(normed_own, "tp", axis=0, tiled=True)
    first_item = lane_index * item_count
    starts = lax.dynamic_slice(item_start, (seq_index, first_item), (1, item_count))[0]
    lengths = lax.dynamic_slice(item_len, (seq_index, first_item), (1, item_count))[0]
    owners = lax.dynamic_slice(item_owner, (seq_index, first_item), (1, item_count))[0]
    outgoing = outgoing_rows(
        grad_res, starts, lengths, owners, lane_index * tok_rows, seq_count, slot_rows
    )
    incoming = lax.all_to_all(outgoing, "seq", split_axis=0, concat_axis=0, tiled=True)
    owner_table = lax.dynamic_slice_in_dim(item_owner, first_item, item_count, 1)
    length_table = lax.dynamic_slice_in_dim(item_len, first_item, item_count, 1)
    own_block = compact_rows(incoming, owner_table, length_table, seq_index, own_rows)
    routed = lax.all_gather(own_block, "tp", axis=0, tiled=True)
    pre_act = jnp.dot(normed, hidden_proj, preferred_element_type=jnp.float32)
    activated = jax.nn.gelu(pre_act, approximate=False).astype(jnp.bfloat16)
    grad_act = jnp.einsum("rd,hd->rh", routed, output_proj, preferred_element_type=jnp.float32)
    grad_pre = (grad_act * gelu_slope(pre_act)).astype(jnp.bfloat16)
    full_term = jnp.einsum("rh,mh->rm", grad_pre, hidden_proj, preferred_element_type=jnp.float32)
    summed = lax.psum(full_term.astype(jnp.bfloat16), "tp").astype(jnp.float32)
    own_grad = lax.dynamic_slice_in_dim(summed, lane_index * own_rows, own_rows, 0)
    scaled = own_grad * norm_gain
    grad_mean = jnp.mean(scaled, axis=1, keepdims=True)
    cross_mean = jnp.mean(scaled * unit_rows, axis=1, keepdims=True)
    feat_grad = ((scaled - grad_mean - unit_rows * cross_mean) * inv_std).astype(jnp.bfloat16)
    inverse = 1.0 / seq_count
    columns = normed
    grad_hidden = (
        lax.psum_scatter(
            jnp.einsum("rm,rh->mh", columns, grad_pre, preferred_element_type=jnp.float32).astype(
                jnp.bfloat16
            ),
            "seq",
            scatter_dimension=0,
            tiled=True,
        ).astype(jnp.float32)
        * inverse
    )
    columns = routed
    grad_output = (
        lax.psum_scatter(
            jnp.einsum("rd,rh->dh", columns, activated, preferred_element_type=jnp.float32).astype(
                jnp.bfloat16
            ),
            "seq",
            scatter_dimension=0,
            tiled=True,
        ).astype(jnp.float32)
        * inverse
    )
    return (feat_grad, grad_hidden, grad_output)


def pack_rows(grad_res, starts, lengths, base_row, own_rows):
    item_count = lengths.shape[0]
    longest = own_rows // item_count
    step = jnp.arange(longest, dtype=jnp.int32)[None, :]
    source = jnp.where(step < lengths[:, None], starts[:, None] - base_row + step, -1)
    chosen = source.reshape(-1, 1) == jnp.arange(grad_res.shape[0], dtype=jnp.int32)[None, :]
    return jnp.dot(
        chosen.astype(jnp.bfloat16), grad_res, preferred_element_type=jnp.float32
    ).astype(jnp.bfloat16)


def destinations(item_len, item_owner, seq_count, lane_count, own_rows):
    item_count = item_len.shape[1] // lane_count
    longest = own_rows // item_count
    shape = (seq_count, lane_count, item_count)
    lengths = jnp.transpose(item_len.reshape(shape), (1, 0, 2)).reshape(lane_count, -1)
    owners = jnp.transpose(item_owner.reshape(shape), (1, 0, 2)).reshape(lane_count, -1)
    order = jnp.arange(seq_count * item_count)
    before = (owners[:, :, None] == owners[:, None, :]) & (order[None, :] < order[:, None])
    offset = jnp.sum(jnp.where(before, lengths[:, None, :], 0), axis=2)
    first = (owners * lane_count + jnp.arange(lane_count)[:, None]) * own_rows + offset
    step = jnp.arange(longest)
    target = jnp.where(step < lengths[:, :, None], first[:, :, None] + step, -1)
    target = target.reshape(lane_count, seq_count, item_count * longest)
    return jnp.transpose(target, (1, 0, 2)).reshape(-1)


def per_device_gathered(
    grad_res, features, norm_gain, hidden_proj, output_proj, item_start, item_len, item_owner
):
    seq_count = lax.axis_size("seq")
    lane_count = lax.axis_size("tp")
    seq_index = lax.axis_index("seq")
    lane_index = lax.axis_index("tp")
    tok_rows = grad_res.shape[0]
    own_rows = features.shape[0]
    item_count = item_len.shape[1] // lane_count
    owner_rows = own_rows * lane_count
    values = features.astype(jnp.float32)
    row_mean = jnp.mean(values, axis=1, keepdims=True)
    centered = values - row_mean
    variance = jnp.mean(centered * centered, axis=1, keepdims=True)
    inv_std = lax.rsqrt(variance + EPSILON)
    unit_rows = centered * inv_std
    normed_own = (unit_rows * norm_gain).astype(jnp.bfloat16)
    first_item = lane_index * item_count
    starts = lax.dynamic_slice(item_start, (seq_index, first_item), (1, item_count))[0]
    lengths = lax.dynamic_slice(item_len, (seq_index, first_item), (1, item_count))[0]
    packed = pack_rows(grad_res, starts, lengths, lane_index * tok_rows, own_rows)
    normed = lax.all_gather(normed_own, ("seq", "tp"), axis=0, tiled=True)
    gathered = lax.all_gather(packed, ("seq", "tp"), axis=0, tiled=True)
    target = destinations(item_len, item_owner, seq_count, lane_count, own_rows)
    place = jnp.arange(target.shape[0])[:, None] == target[None, :]
    routed = jnp.dot(
        place.astype(jnp.bfloat16), gathered, preferred_element_type=jnp.float32
    ).astype(jnp.bfloat16)
    pre_act = jnp.dot(normed, hidden_proj, preferred_element_type=jnp.float32)
    activated = jax.nn.gelu(pre_act, approximate=False).astype(jnp.bfloat16)
    grad_act = jnp.einsum("rd,hd->rh", routed, output_proj, preferred_element_type=jnp.float32)
    grad_pre = (grad_act * gelu_slope(pre_act)).astype(jnp.bfloat16)
    own_pre = lax.dynamic_slice_in_dim(grad_pre, seq_index * owner_rows, owner_rows, 0)
    full_term = jnp.einsum("rh,mh->rm", own_pre, hidden_proj, preferred_element_type=jnp.float32)
    own_grad = lax.psum_scatter(
        full_term.astype(jnp.bfloat16), "tp", scatter_dimension=0, tiled=True
    ).astype(jnp.float32)
    scaled = own_grad * norm_gain
    grad_mean = jnp.mean(scaled, axis=1, keepdims=True)
    cross_mean = jnp.mean(scaled * unit_rows, axis=1, keepdims=True)
    feat_grad = ((scaled - grad_mean - unit_rows * cross_mean) * inv_std).astype(jnp.bfloat16)
    inverse = 1.0 / seq_count
    m_cut = normed.shape[1] // seq_count
    d_cut = routed.shape[1] // seq_count
    normed_cut = lax.dynamic_slice_in_dim(normed, seq_index * m_cut, m_cut, 1)
    routed_cut = lax.dynamic_slice_in_dim(routed, seq_index * d_cut, d_cut, 1)
    grad_hidden = (
        jnp.einsum("rm,rh->mh", normed_cut, grad_pre, preferred_element_type=jnp.float32) * inverse
    )
    grad_output = (
        jnp.einsum("rd,rh->dh", routed_cut, activated, preferred_element_type=jnp.float32) * inverse
    )
    return (feat_grad, grad_hidden, grad_output)


def solution(mesh):
    body = per_device_gathered if mesh.shape["seq"] <= 4 else per_device
    in_specs = (
        P(("grp", "seq", "tp"), None),
        P(("grp", "seq", "tp"), None),
        P(),
        P(None, "tp"),
        P("tp", None),
        P("grp", None),
        P("grp", None),
        P("grp", None),
    )
    out_specs = (P(("grp", "seq", "tp"), None), P(("grp", "seq"), "tp"), P(("grp", "seq"), "tp"))
    return jax.shard_map(
        body, mesh=mesh, in_specs=in_specs, out_specs=out_specs, check_vma=False
    )
```

```python
import jax
import jax.numpy as jnp
from jax import lax
from jax.experimental import pallas as pl
from jax.experimental.pallas import tpu as pltpu
from jax.sharding import PartitionSpec as P

EPSILON = 1e-06


def gelu_slope(pre_act):
    normal_cdf = 0.5 * (1.0 + lax.erf(pre_act * 0.7071067811865476))
    density = jnp.exp(-0.5 * pre_act * pre_act) * 0.3989422804014327
    return normal_cdf + pre_act * density


def outgoing_rows(grad_res, starts, lengths, owners, base_row, seq_count, slot_rows):
    item_count = owners.shape[0]
    order_index = jnp.arange(item_count)
    same_owner = owners[:, None] == owners[None, :]
    earlier = order_index[None, :] < order_index[:, None]
    offset = jnp.sum(jnp.where(same_owner & earlier, lengths[None, :], 0), axis=1)
    destination = jnp.arange(seq_count)[:, None, None]
    place_index = jnp.arange(slot_rows)[None, :, None]
    matched = (
        (owners[None, None, :] == destination)
        & (place_index >= offset)
        & (place_index < offset + lengths)
    )
    local_row = starts - base_row + place_index - offset
    source_row = jnp.sum(jnp.where(matched, local_row, 0), axis=2).reshape(-1)
    filled = jnp.any(matched, axis=2).reshape(-1, 1)
    picked = jnp.take(grad_res, source_row, axis=0)
    picked = jnp.where(filled, picked, jnp.zeros((), picked.dtype))
    return picked.reshape(seq_count, slot_rows, grad_res.shape[1])


def compact_rows(incoming, owner_table, length_table, seq_index, own_rows):
    seq_count, slot_rows, model_width = incoming.shape
    counts = jnp.sum(jnp.where(owner_table == seq_index, length_table, 0), axis=1)
    starts_at = jnp.cumsum(counts) - counts
    position = jnp.arange(own_rows)[:, None]
    inside = (position >= starts_at[None, :]) & (position < (starts_at + counts)[None, :])
    flat_index = jnp.arange(seq_count)[None, :] * slot_rows + position - starts_at[None, :]
    slot_index = jnp.sum(jnp.where(inside, flat_index, 0), axis=1)
    present = jnp.any(inside, axis=1)[:, None]
    gathered = jnp.take(incoming.reshape(seq_count * slot_rows, model_width), slot_index, axis=0)
    return jnp.where(present, gathered, jnp.zeros((), gathered.dtype))


def per_device(
    grad_res, features, norm_gain, hidden_proj, output_proj, item_start, item_len, item_owner
):
    seq_count = lax.axis_size("seq")
    lane_count = lax.axis_size("tp")
    seq_index = lax.axis_index("seq")
    lane_index = lax.axis_index("tp")
    tok_rows = grad_res.shape[0]
    own_rows = features.shape[0]
    item_count = item_len.shape[1] // lane_count
    longest = own_rows // item_count
    slot_rows = longest * max(1, item_count // seq_count)
    values = features.astype(jnp.float32)
    row_mean = jnp.mean(values, axis=1, keepdims=True)
    centered = values - row_mean
    variance = jnp.mean(centered * centered, axis=1, keepdims=True)
    inv_std = lax.rsqrt(variance + EPSILON)
    unit_rows = centered * inv_std
    normed_own = (unit_rows * norm_gain).astype(jnp.bfloat16)
    normed = lax.all_gather(normed_own, "tp", axis=0, tiled=True)
    first_item = lane_index * item_count
    starts = lax.dynamic_slice(item_start, (seq_index, first_item), (1, item_count))[0]
    lengths = lax.dynamic_slice(item_len, (seq_index, first_item), (1, item_count))[0]
    owners = lax.dynamic_slice(item_owner, (seq_index, first_item), (1, item_count))[0]
    outgoing = outgoing_rows(
        grad_res, starts, lengths, owners, lane_index * tok_rows, seq_count, slot_rows
    )
    incoming = lax.all_to_all(outgoing, "seq", split_axis=0, concat_axis=0, tiled=True)
    owner_table = lax.dynamic_slice_in_dim(item_owner, first_item, item_count, 1)
    length_table = lax.dynamic_slice_in_dim(item_len, first_item, item_count, 1)
    own_block = compact_rows(incoming, owner_table, length_table, seq_index, own_rows)
    routed = lax.all_gather(own_block, "tp", axis=0, tiled=True)
    pre_act = jnp.dot(normed, hidden_proj, preferred_element_type=jnp.float32)
    activated = jax.nn.gelu(pre_act, approximate=False).astype(jnp.bfloat16)
    grad_act = jnp.einsum("rd,hd->rh", routed, output_proj, preferred_element_type=jnp.float32)
    grad_pre = (grad_act * gelu_slope(pre_act)).astype(jnp.bfloat16)
    full_term = jnp.einsum("rh,mh->rm", grad_pre, hidden_proj, preferred_element_type=jnp.float32)
    summed = lax.psum(full_term.astype(jnp.bfloat16), "tp").astype(jnp.float32)
    own_grad = lax.dynamic_slice_in_dim(summed, lane_index * own_rows, own_rows, 0)
    scaled = own_grad * norm_gain
    grad_mean = jnp.mean(scaled, axis=1, keepdims=True)
    cross_mean = jnp.mean(scaled * unit_rows, axis=1, keepdims=True)
    feat_grad = ((scaled - grad_mean - unit_rows * cross_mean) * inv_std).astype(jnp.bfloat16)
    inverse = 1.0 / seq_count
    columns = normed
    grad_hidden = (
        lax.psum_scatter(
            jnp.einsum("rm,rh->mh", columns, grad_pre, preferred_element_type=jnp.float32).astype(
                jnp.bfloat16
            ),
            "seq",
            scatter_dimension=0,
            tiled=True,
        ).astype(jnp.float32)
        * inverse
    )
    columns = routed
    grad_output = (
        lax.psum_scatter(
            jnp.einsum("rd,rh->dh", columns, activated, preferred_element_type=jnp.float32).astype(
                jnp.bfloat16
            ),
            "seq",
            scatter_dimension=0,
            tiled=True,
        ).astype(jnp.float32)
        * inverse
    )
    return (feat_grad, grad_hidden, grad_output)


def pack_rows(grad_res, starts, lengths, base_row, own_rows):
    item_count = lengths.shape[0]
    longest = own_rows // item_count
    step = jnp.arange(longest, dtype=jnp.int32)[None, :]
    source = jnp.where(step < lengths[:, None], starts[:, None] - base_row + step, -1)
    chosen = source.reshape(-1, 1) == jnp.arange(grad_res.shape[0], dtype=jnp.int32)[None, :]
    return jnp.dot(
        chosen.astype(jnp.bfloat16), grad_res, preferred_element_type=jnp.float32
    ).astype(jnp.bfloat16)


def destinations(item_len, item_owner, seq_count, lane_count, own_rows):
    item_count = item_len.shape[1] // lane_count
    longest = own_rows // item_count
    shape = (seq_count, lane_count, item_count)
    lengths = jnp.transpose(item_len.reshape(shape), (1, 0, 2)).reshape(lane_count, -1)
    owners = jnp.transpose(item_owner.reshape(shape), (1, 0, 2)).reshape(lane_count, -1)
    order = jnp.arange(seq_count * item_count)
    before = (owners[:, :, None] == owners[:, None, :]) & (order[None, :] < order[:, None])
    offset = jnp.sum(jnp.where(before, lengths[:, None, :], 0), axis=2)
    first = owners * own_rows + offset
    step = jnp.arange(longest)
    target = jnp.where(step < lengths[:, :, None], first[:, :, None] + step, -1)
    return target.reshape(lane_count, seq_count * item_count * longest)


MESH = pl.DeviceIdType.MESH
UP, DOWN, ACROSS, SIBLING, RELAY = range(5)


def dot_nt(lhs, rhs):
    return lax.dot_general(lhs, rhs, (((1,), (1,)), ((), ())), preferred_element_type=jnp.float32)


def exchange_kernel(
    normed_ref,
    packed_ref,
    place_ref,
    hidden_hbm,
    output_hbm,
    grad_pre_ref,
    active_ref,
    normed_cut_ref,
    routed_cut_ref,
    own_grad_ref,
    hidden_w,
    output_w,
    normed_all,
    packed_all,
    routed_all,
    partial,
    from_sibling,
    to_across,
    from_across,
    load_sem,
    send_sem,
    recv_sem,
    sum_send,
    sum_recv,
):
    seq_count, lane_rows, m_width = normed_all.shape
    rows = normed_ref.shape[0]
    d_width = packed_ref.shape[1]
    h_width = hidden_w.shape[1]
    grp = lax.axis_index("grp")
    me = lax.axis_index("seq")
    lane = lax.axis_index("tp")
    chip, core = lane // 2, lane % 2
    sibling = chip * 2 + (1 - core)
    across = (1 - chip) * 2 + core
    diagonal = (1 - chip) * 2 + (1 - core)
    last = seq_count - 1
    has_up, has_down = me < last, me > 0

    load_hidden = pltpu.make_async_copy(hidden_hbm, hidden_w, load_sem.at[0])
    load_output = pltpu.make_async_copy(output_hbm, output_w, load_sem.at[1])
    load_hidden.start()
    load_output.start()

    barrier = pltpu.get_barrier_semaphore()

    def greet(seq_to, lane_to):
        pl.semaphore_signal(
            barrier, inc=1, device_id=(grp, seq_to, lane_to), device_id_type=MESH
        )

    greet(me, sibling)
    greet(me, across)

    @pl.when(has_up)
    def _():
        greet(me + 1, lane)

    @pl.when(has_down)
    def _():
        greet(me - 1, lane)

    pl.semaphore_wait(barrier, jnp.where((me == 0) | (me == last), 3, 4))

    def slot(kind, plane, lane_at):
        if kind == 0:
            return normed_all.at[plane, pl.ds(pl.multiple_of(lane_at * rows, 16), rows)]
        return packed_all.at[lane_at, pl.ds(pl.multiple_of(plane * rows, 16), rows)]

    def copy(kind, plane, lane_at, way):
        target = {
            UP: (grp, jnp.minimum(me + 1, last), lane),
            DOWN: (grp, jnp.maximum(me - 1, 0), lane),
            ACROSS: (grp, me, across),
            SIBLING: (grp, me, sibling),
            RELAY: (grp, me, sibling),
        }[way]
        return pltpu.make_async_remote_copy(
            src_ref=slot(kind, plane, lane_at),
            dst_ref=slot(kind, plane, lane_at),
            send_sem=send_sem.at[kind, way, plane],
            recv_sem=recv_sem.at[kind, plane, lane_at],
            device_id=target,
            device_id_type=MESH,
        )

    def arrived(kind, plane, lane_at):
        copy(kind, plane, lane_at, SIBLING).wait_recv()

    mirrored = me >= seq_count // 2
    near = jnp.where(mirrored, last - me, me)

    def plane_at(step):
        place = jnp.where((step < 2) & (near == 1), 1 - step, step)
        return jnp.where(mirrored, last - place, place)

    def along_seq(kind):
        @pl.when(has_up)
        def _():
            copy(kind, me, lane, UP).start()

        @pl.when(has_down)
        def _():
            copy(kind, me, lane, DOWN).start()

    def own_out(kind):
        copy(kind, me, lane, ACROSS).start()
        copy(kind, me, lane, SIBLING).start()

    def seq_stage(kind, step):
        plane = plane_at(step)
        arrived(kind, plane, lane)

        @pl.when((plane < me) & has_up)
        def _():
            copy(kind, plane, lane, UP).start()

        @pl.when((plane > me) & has_down)
        def _():
            copy(kind, plane, lane, DOWN).start()

        copy(kind, plane, lane, ACROSS).start()
        copy(kind, plane, lane, SIBLING).start()

    def across_stage(kind, step):
        plane = plane_at(step)
        arrived(kind, plane, across)
        copy(kind, plane, across, RELAY).start()

    def sibling_stage(kind, step):
        plane = plane_at(step)
        arrived(kind, plane, sibling)
        arrived(kind, plane, diagonal)

    h_tile = h_width // 3

    def activate(plane):
        base = pl.multiple_of(plane * lane_rows, 16)

        @pl.loop(0, 3)
        def _(tile):
            cols = pl.ds(pl.multiple_of(tile * h_tile, 128), h_tile)
            pre_act = jnp.dot(
                normed_all[plane], hidden_w[:, cols], preferred_element_type=jnp.float32
            )
            grad_act = dot_nt(routed_all[plane], output_w[cols, :])
            normal_cdf = 0.5 * (1.0 + lax.erf(pre_act * 0.7071067811865476))
            density = jnp.exp(-0.5 * pre_act * pre_act) * 0.3989422804014327
            active_ref[pl.ds(base, lane_rows), cols] = (pre_act * normal_cdf).astype(jnp.bfloat16)
            grad_pre_ref[pl.ds(base, lane_rows), cols] = (
                grad_act * (normal_cdf + pre_act * density)
            ).astype(jnp.bfloat16)

    def place_rows():
        width = d_width // 8

        @pl.loop(0, 8)
        def _(tile):
            cols = pl.ds(pl.multiple_of(tile * width, 128), width)
            for lane_at in range(place_ref.shape[0]):
                placed = jnp.dot(
                    place_ref[lane_at],
                    packed_all[lane_at, :, cols],
                    preferred_element_type=jnp.float32,
                ).astype(jnp.bfloat16)
                for owner in range(seq_count):
                    routed_all[owner, lane_at * rows : (lane_at + 1) * rows, cols] = placed[
                        owner * rows : (owner + 1) * rows
                    ]

    def partial_rows(lane_at):
        return partial.at[pl.ds(pl.multiple_of(lane_at * rows, 16), rows)]

    def sum_copy(index):
        source, target, lane_to = (
            (partial_rows(sibling), from_sibling.at[0], sibling),
            (partial_rows(diagonal), from_sibling.at[1], sibling),
            (to_across, from_across, across),
        )[index]
        return pltpu.make_async_remote_copy(
            src_ref=source,
            dst_ref=target,
            send_sem=sum_send.at[index],
            recv_sem=sum_recv.at[index],
            device_id=(grp, me, lane_to),
            device_id_type=MESH,
        )

    def own_partial():
        own_pre = pl.ds(pl.multiple_of(me * lane_rows, 16), lane_rows)
        width = m_width // 9

        @pl.loop(0, 9)
        def _(tile):
            cols = pl.ds(pl.multiple_of(tile * width, 128), width)
            partial[:, cols] = dot_nt(grad_pre_ref[own_pre, :], hidden_w[cols, :]).astype(
                jnp.bfloat16
            )

    normed_all[me, pl.ds(pl.multiple_of(lane * rows, 16), rows), :] = normed_ref[...]
    packed_all[lane, pl.ds(pl.multiple_of(me * rows, 16), rows), :] = packed_ref[...]

    own_out(1)
    along_seq(1)
    own_out(0)
    seq_stage(1, 1)
    along_seq(0)
    across_stage(1, 0)
    across_stage(0, 0)
    sibling_stage(1, 0)
    sibling_stage(0, 0)
    for step in range(2, seq_count):
        seq_stage(1, step)
        across_stage(1, step - 1)
        sibling_stage(1, step - 1)
    seq_stage(0, 1)
    across_stage(1, last)
    seq_stage(0, 2)
    sibling_stage(1, last)
    place_rows()
    across_stage(0, 1)
    load_hidden.wait()
    load_output.wait()
    activate(me)
    own_partial()
    sum_copy(0).start()
    sum_copy(1).start()
    seq_stage(0, 3)
    across_stage(0, 2)
    sibling_stage(0, 1)
    activate(plane_at(1))
    sum_copy(1).wait_recv()
    to_across[...] = (
        partial_rows(across)[...].astype(jnp.float32) + from_sibling[1].astype(jnp.float32)
    ).astype(jnp.bfloat16)
    sum_copy(2).start()
    sibling_stage(0, 2)
    activate(plane_at(2))
    d_cut = routed_cut_ref.shape[1]
    for owner in range(seq_count):
        routed_cut_ref[owner * lane_rows : (owner + 1) * lane_rows, :] = routed_all[
            owner, :, pl.ds(pl.multiple_of(me * d_cut, 128), d_cut)
        ]
    across_stage(0, 3)
    sibling_stage(0, 3)
    activate(plane_at(3))
    m_cut = normed_cut_ref.shape[1]
    for owner in range(seq_count):
        normed_cut_ref[owner * lane_rows : (owner + 1) * lane_rows, :] = normed_all[
            owner, :, pl.ds(pl.multiple_of(me * m_cut, 128), m_cut)
        ]
    sum_copy(0).wait_recv()
    sum_copy(2).wait_recv()
    own_grad_ref[...] = (
        partial_rows(lane)[...].astype(jnp.float32)
        + from_sibling[0].astype(jnp.float32)
        + from_across[...].astype(jnp.float32)
    )

    for index in range(3):
        sum_copy(index).wait_send()
    for kind in (0, 1):
        @pl.when(has_up)
        def _():
            copy(kind, me, lane, UP).wait_send()

        @pl.when(has_down)
        def _():
            copy(kind, me, lane, DOWN).wait_send()

        for step in range(seq_count):
            plane = plane_at(step)
            if step:
                @pl.when((plane < me) & has_up)
                def _():
                    copy(kind, plane, lane, UP).wait_send()

                @pl.when((plane > me) & has_down)
                def _():
                    copy(kind, plane, lane, DOWN).wait_send()

            copy(kind, plane, lane, ACROSS).wait_send()
            copy(kind, plane, lane, SIBLING).wait_send()
            copy(kind, plane, across, RELAY).wait_send()


def exchange(normed_own, packed, place, hidden_proj, output_proj, seq_count):
    rows, m_width = normed_own.shape
    d_width = packed.shape[1]
    h_width = hidden_proj.shape[1]
    lane_count = place.shape[0]
    lane_rows = rows * lane_count
    all_rows = lane_rows * seq_count
    vmem = pl.BlockSpec(memory_space=pltpu.VMEM)
    anywhere = pl.BlockSpec(memory_space=pl.ANY)
    shape = jax.ShapeDtypeStruct
    half = jnp.bfloat16
    return pl.pallas_call(
        exchange_kernel,
        out_shape=(
            shape((all_rows, h_width), half),
            shape((all_rows, h_width), half),
            shape((all_rows, m_width // seq_count), half),
            shape((all_rows, d_width // seq_count), half),
            shape((rows, m_width), jnp.float32),
        ),
        in_specs=[vmem, vmem, vmem, anywhere, anywhere],
        out_specs=(vmem,) * 5,
        scratch_shapes=[
            pltpu.VMEM((m_width, h_width), half),
            pltpu.VMEM((h_width, d_width), half),
            pltpu.VMEM((seq_count, lane_rows, m_width), half),
            pltpu.VMEM((lane_count, seq_count * rows, d_width), half),
            pltpu.VMEM((seq_count, lane_rows, d_width), half),
            pltpu.VMEM((lane_rows, m_width), half),
            pltpu.VMEM((2, rows, m_width), half),
            pltpu.VMEM((rows, m_width), half),
            pltpu.VMEM((rows, m_width), half),
            pltpu.SemaphoreType.DMA((2,)),
            pltpu.SemaphoreType.DMA((2, 5, seq_count)),
            pltpu.SemaphoreType.DMA((2, seq_count, lane_count)),
            pltpu.SemaphoreType.DMA((3,)),
            pltpu.SemaphoreType.DMA((3,)),
        ],
        compiler_params=pltpu.CompilerParams(
            collective_id=0, has_side_effects=True, vmem_limit_bytes=60 * 1024 * 1024
        ),
        cost_estimate=pl.CostEstimate(
            flops=2 * all_rows * h_width * (m_width + d_width),
            bytes_accessed=2 * h_width * (m_width + d_width),
            transcendentals=2 * all_rows * h_width,
        ),
    )(normed_own, packed, place, hidden_proj, output_proj)


def per_device_gathered(
    grad_res, features, norm_gain, hidden_proj, output_proj, item_start, item_len, item_owner
):
    seq_count = lax.axis_size("seq")
    lane_count = lax.axis_size("tp")
    seq_index = lax.axis_index("seq")
    lane_index = lax.axis_index("tp")
    tok_rows = grad_res.shape[0]
    own_rows = features.shape[0]
    item_count = item_len.shape[1] // lane_count
    values = features.astype(jnp.float32)
    row_mean = jnp.mean(values, axis=1, keepdims=True)
    centered = values - row_mean
    variance = jnp.mean(centered * centered, axis=1, keepdims=True)
    inv_std = lax.rsqrt(variance + EPSILON)
    unit_rows = centered * inv_std
    normed_own = (unit_rows * norm_gain).astype(jnp.bfloat16)
    first_item = lane_index * item_count
    starts = lax.dynamic_slice(item_start, (seq_index, first_item), (1, item_count))[0]
    lengths = lax.dynamic_slice(item_len, (seq_index, first_item), (1, item_count))[0]
    packed = pack_rows(grad_res, starts, lengths, lane_index * tok_rows, own_rows)
    target = destinations(item_len, item_owner, seq_count, lane_count, own_rows)
    place = jnp.arange(seq_count * own_rows)[None, :, None] == target[:, None, :]
    grad_pre, activated, normed_cut, routed_cut, own_grad = exchange(
        normed_own, packed, place.astype(jnp.bfloat16), hidden_proj, output_proj, seq_count
    )
    scaled = own_grad * norm_gain
    grad_mean = jnp.mean(scaled, axis=1, keepdims=True)
    cross_mean = jnp.mean(scaled * unit_rows, axis=1, keepdims=True)
    feat_grad = ((scaled - grad_mean - unit_rows * cross_mean) * inv_std).astype(jnp.bfloat16)
    inverse = 1.0 / seq_count
    grad_hidden = (
        jnp.einsum("rm,rh->mh", normed_cut, grad_pre, preferred_element_type=jnp.float32) * inverse
    )
    grad_output = (
        jnp.einsum("rd,rh->dh", routed_cut, activated, preferred_element_type=jnp.float32) * inverse
    )
    return (feat_grad, grad_hidden, grad_output)


def solution(mesh):
    body = per_device_gathered if (mesh.shape["seq"], mesh.shape["tp"]) == (4, 4) else per_device
    in_specs = (
        P(("grp", "seq", "tp"), None),
        P(("grp", "seq", "tp"), None),
        P(),
        P(None, "tp"),
        P("tp", None),
        P("grp", None),
        P("grp", None),
        P("grp", None),
    )
    out_specs = (P(("grp", "seq", "tp"), None), P(("grp", "seq"), "tp"), P(("grp", "seq"), "tp"))
    return jax.shard_map(
        body, mesh=mesh, in_specs=in_specs, out_specs=out_specs, check_vma=False
    )
```

```python
import jax
import jax.numpy as jnp
from jax import lax
from jax.experimental import pallas as pl
from jax.experimental.pallas import tpu as pltpu
from jax.sharding import PartitionSpec as P

EPSILON = 1e-06


def gelu_slope(pre_act):
    normal_cdf = 0.5 * (1.0 + lax.erf(pre_act * 0.7071067811865476))
    density = jnp.exp(-0.5 * pre_act * pre_act) * 0.3989422804014327
    return normal_cdf + pre_act * density


def outgoing_rows(grad_res, starts, lengths, owners, base_row, seq_count, slot_rows):
    item_count = owners.shape[0]
    order_index = jnp.arange(item_count)
    same_owner = owners[:, None] == owners[None, :]
    earlier = order_index[None, :] < order_index[:, None]
    offset = jnp.sum(jnp.where(same_owner & earlier, lengths[None, :], 0), axis=1)
    destination = jnp.arange(seq_count)[:, None, None]
    place_index = jnp.arange(slot_rows)[None, :, None]
    matched = (
        (owners[None, None, :] == destination)
        & (place_index >= offset)
        & (place_index < offset + lengths)
    )
    local_row = starts - base_row + place_index - offset
    source_row = jnp.sum(jnp.where(matched, local_row, 0), axis=2).reshape(-1)
    filled = jnp.any(matched, axis=2).reshape(-1, 1)
    picked = jnp.take(grad_res, source_row, axis=0)
    picked = jnp.where(filled, picked, jnp.zeros((), picked.dtype))
    return picked.reshape(seq_count, slot_rows, grad_res.shape[1])


def compact_rows(incoming, owner_table, length_table, seq_index, own_rows):
    seq_count, slot_rows, model_width = incoming.shape
    counts = jnp.sum(jnp.where(owner_table == seq_index, length_table, 0), axis=1)
    starts_at = jnp.cumsum(counts) - counts
    position = jnp.arange(own_rows)[:, None]
    inside = (position >= starts_at[None, :]) & (position < (starts_at + counts)[None, :])
    flat_index = jnp.arange(seq_count)[None, :] * slot_rows + position - starts_at[None, :]
    slot_index = jnp.sum(jnp.where(inside, flat_index, 0), axis=1)
    present = jnp.any(inside, axis=1)[:, None]
    gathered = jnp.take(incoming.reshape(seq_count * slot_rows, model_width), slot_index, axis=0)
    return jnp.where(present, gathered, jnp.zeros((), gathered.dtype))


def per_device(
    grad_res, features, norm_gain, hidden_proj, output_proj, item_start, item_len, item_owner
):
    seq_count = lax.axis_size("seq")
    lane_count = lax.axis_size("tp")
    seq_index = lax.axis_index("seq")
    lane_index = lax.axis_index("tp")
    tok_rows = grad_res.shape[0]
    own_rows = features.shape[0]
    item_count = item_len.shape[1] // lane_count
    longest = own_rows // item_count
    slot_rows = longest * max(1, item_count // seq_count)
    values = features.astype(jnp.float32)
    row_mean = jnp.mean(values, axis=1, keepdims=True)
    centered = values - row_mean
    variance = jnp.mean(centered * centered, axis=1, keepdims=True)
    inv_std = lax.rsqrt(variance + EPSILON)
    unit_rows = centered * inv_std
    normed_own = (unit_rows * norm_gain).astype(jnp.bfloat16)
    normed = lax.all_gather(normed_own, "tp", axis=0, tiled=True)
    first_item = lane_index * item_count
    starts = lax.dynamic_slice(item_start, (seq_index, first_item), (1, item_count))[0]
    lengths = lax.dynamic_slice(item_len, (seq_index, first_item), (1, item_count))[0]
    owners = lax.dynamic_slice(item_owner, (seq_index, first_item), (1, item_count))[0]
    outgoing = outgoing_rows(
        grad_res, starts, lengths, owners, lane_index * tok_rows, seq_count, slot_rows
    )
    incoming = lax.all_to_all(outgoing, "seq", split_axis=0, concat_axis=0, tiled=True)
    owner_table = lax.dynamic_slice_in_dim(item_owner, first_item, item_count, 1)
    length_table = lax.dynamic_slice_in_dim(item_len, first_item, item_count, 1)
    own_block = compact_rows(incoming, owner_table, length_table, seq_index, own_rows)
    routed = lax.all_gather(own_block, "tp", axis=0, tiled=True)
    pre_act = jnp.dot(normed, hidden_proj, preferred_element_type=jnp.float32)
    activated = jax.nn.gelu(pre_act, approximate=False).astype(jnp.bfloat16)
    grad_act = jnp.einsum("rd,hd->rh", routed, output_proj, preferred_element_type=jnp.float32)
    grad_pre = (grad_act * gelu_slope(pre_act)).astype(jnp.bfloat16)
    full_term = jnp.einsum("rh,mh->rm", grad_pre, hidden_proj, preferred_element_type=jnp.float32)
    summed = lax.psum(full_term.astype(jnp.bfloat16), "tp").astype(jnp.float32)
    own_grad = lax.dynamic_slice_in_dim(summed, lane_index * own_rows, own_rows, 0)
    scaled = own_grad * norm_gain
    grad_mean = jnp.mean(scaled, axis=1, keepdims=True)
    cross_mean = jnp.mean(scaled * unit_rows, axis=1, keepdims=True)
    feat_grad = ((scaled - grad_mean - unit_rows * cross_mean) * inv_std).astype(jnp.bfloat16)
    inverse = 1.0 / seq_count
    columns = normed
    grad_hidden = (
        lax.psum_scatter(
            jnp.einsum("rm,rh->mh", columns, grad_pre, preferred_element_type=jnp.float32).astype(
                jnp.bfloat16
            ),
            "seq",
            scatter_dimension=0,
            tiled=True,
        ).astype(jnp.float32)
        * inverse
    )
    columns = routed
    grad_output = (
        lax.psum_scatter(
            jnp.einsum("rd,rh->dh", columns, activated, preferred_element_type=jnp.float32).astype(
                jnp.bfloat16
            ),
            "seq",
            scatter_dimension=0,
            tiled=True,
        ).astype(jnp.float32)
        * inverse
    )
    return (feat_grad, grad_hidden, grad_output)


def chosen_rows(starts, lengths, base_row, tok_rows, own_rows):
    item_count = lengths.shape[0]
    longest = own_rows // item_count
    step = jnp.arange(longest, dtype=jnp.int32)[None, :]
    source = jnp.where(step < lengths[:, None], starts[:, None] - base_row + step, -1)
    chosen = source.reshape(-1, 1) == jnp.arange(tok_rows, dtype=jnp.int32)[None, :]
    return chosen.astype(jnp.bfloat16)


def destinations(item_len, item_owner, seq_count, lane_count, own_rows):
    item_count = item_len.shape[1] // lane_count
    longest = own_rows // item_count
    shape = (seq_count, lane_count, item_count)
    lengths = jnp.transpose(item_len.reshape(shape), (1, 0, 2)).reshape(lane_count, -1)
    owners = jnp.transpose(item_owner.reshape(shape), (1, 0, 2)).reshape(lane_count, -1)
    order = jnp.arange(seq_count * item_count)
    before = (owners[:, :, None] == owners[:, None, :]) & (order[None, :] < order[:, None])
    offset = jnp.sum(jnp.where(before, lengths[:, None, :], 0), axis=2)
    first = owners * own_rows + offset
    step = jnp.arange(longest)
    target = jnp.where(step < lengths[:, :, None], first[:, :, None] + step, -1)
    return target.reshape(lane_count, seq_count * item_count * longest)


MESH = pl.DeviceIdType.MESH
UP, DOWN, ACROSS, SIBLING, RELAY, PAIR = range(6)


def dot_nt(lhs, rhs):
    return lax.dot_general(lhs, rhs, (((1,), (1,)), ((), ())), preferred_element_type=jnp.float32)


def exchange_kernel(
    features_ref,
    gain_ref,
    chosen_ref,
    grad_res_ref,
    place_ref,
    hidden_hbm,
    output_hbm,
    grad_pre_ref,
    active_ref,
    normed_cut_ref,
    routed_cut_ref,
    feat_grad_ref,
    hidden_w,
    output_w,
    normed_all,
    packed_all,
    routed_all,
    partial,
    from_sibling,
    to_across,
    from_across,
    load_sem,
    send_sem,
    recv_sem,
    sum_send,
    sum_recv,
):
    seq_count, lane_rows, m_width = normed_all.shape
    rows = features_ref.shape[0]
    d_width = grad_res_ref.shape[1]
    h_width = hidden_w.shape[1]
    grp = lax.axis_index("grp")
    me = lax.axis_index("seq")
    lane = lax.axis_index("tp")
    chip, core = lane // 2, lane % 2
    sibling = chip * 2 + (1 - core)
    across = (1 - chip) * 2 + core
    diagonal = (1 - chip) * 2 + (1 - core)
    last = seq_count - 1
    has_up, has_down = me < last, me > 0

    load_hidden = pltpu.make_async_copy(hidden_hbm, hidden_w, load_sem.at[0])
    load_output = pltpu.make_async_copy(output_hbm, output_w, load_sem.at[1])
    load_hidden.start()
    load_output.start()

    barrier = pltpu.get_barrier_semaphore()

    def greet(seq_to, lane_to):
        pl.semaphore_signal(
            barrier, inc=1, device_id=(grp, seq_to, lane_to), device_id_type=MESH
        )

    greet(me, sibling)
    greet(me, across)

    @pl.when(has_up)
    def _():
        greet(me + 1, lane)

    @pl.when(has_down)
    def _():
        greet(me - 1, lane)

    pack_width = d_width // 8

    @pl.loop(0, 8)
    def _(tile):
        cols = pl.ds(pl.multiple_of(tile * pack_width, 128), pack_width)
        packed_all[lane, pl.ds(pl.multiple_of(me * rows, 16), rows), cols] = jnp.dot(
            chosen_ref[...], grad_res_ref[:, cols], preferred_element_type=jnp.float32
        ).astype(jnp.bfloat16)

    pl.semaphore_wait(barrier, jnp.where((me == 0) | (me == last), 3, 4))

    def slot(kind, plane, lane_at):
        if kind == 0:
            return normed_all.at[plane, pl.ds(pl.multiple_of(lane_at * rows, 16), rows)]
        return packed_all.at[lane_at, pl.ds(pl.multiple_of(plane * rows, 16), rows)]

    def copy(kind, plane, lane_at, way):
        target = {
            UP: (grp, jnp.minimum(me + 1, last), lane),
            DOWN: (grp, jnp.maximum(me - 1, 0), lane),
            ACROSS: (grp, me, across),
            SIBLING: (grp, me, sibling),
            RELAY: (grp, me, sibling),
            PAIR: (grp, pair, lane),
        }[way]
        return pltpu.make_async_remote_copy(
            src_ref=slot(kind, plane, lane_at),
            dst_ref=slot(kind, plane, lane_at),
            send_sem=send_sem.at[kind, way, plane],
            recv_sem=recv_sem.at[kind, plane, lane_at],
            device_id=target,
            device_id_type=MESH,
        )

    def arrived(kind, plane, lane_at):
        copy(kind, plane, lane_at, SIBLING).wait_recv()

    mirrored = me >= seq_count // 2
    near = jnp.where(mirrored, last - me, me)

    def plane_at(step):
        place = jnp.where((step < 2) & (near == 1), 1 - step, step)
        return jnp.where(mirrored, last - place, place)

    pair = me + 1 - 2 * (me % 2)
    at_end = (me == 0) | (me == last)

    def when_spared(act):
        pl.when(at_end)(act)

    def when_crossed(step, act):
        if step != 1:
            act()
        else:
            pl.when(at_end)(act)

    def along_seq(kind):
        @pl.when(has_up)
        def _():
            copy(kind, me, lane, UP).start()

        @pl.when(has_down)
        def _():
            copy(kind, me, lane, DOWN).start()

    def own_out(kind):
        copy(kind, me, lane, ACROSS).start()
        copy(kind, me, lane, SIBLING).start()

    def seq_stage(kind, step):
        plane = plane_at(step)
        arrived(kind, plane, lane)

        @pl.when((plane < me) & has_up)
        def _():
            copy(kind, plane, lane, UP).start()

        @pl.when((plane > me) & has_down)
        def _():
            copy(kind, plane, lane, DOWN).start()

        when_crossed(step, lambda: copy(kind, plane, lane, ACROSS).start())
        copy(kind, plane, lane, SIBLING).start()

    def across_stage(kind, step):
        plane = plane_at(step)
        arrived(kind, plane, across)
        if step == 0:
            when_spared(lambda: copy(kind, me, across, PAIR).start())
        copy(kind, plane, across, RELAY).start()

    def sibling_stage(kind, step):
        plane = plane_at(step)
        arrived(kind, plane, sibling)
        arrived(kind, plane, diagonal)

    h_tile = h_width // 3

    def activate(plane):
        base = pl.multiple_of(plane * lane_rows, 16)

        @pl.loop(0, 3)
        def _(tile):
            cols = pl.ds(pl.multiple_of(tile * h_tile, 128), h_tile)
            pre_act = jnp.dot(
                normed_all[plane], hidden_w[:, cols], preferred_element_type=jnp.float32
            )
            grad_act = dot_nt(routed_all[plane], output_w[cols, :])
            normal_cdf = 0.5 * (1.0 + lax.erf(pre_act * 0.7071067811865476))
            density = jnp.exp(-0.5 * pre_act * pre_act) * 0.3989422804014327
            active_ref[pl.ds(base, lane_rows), cols] = (pre_act * normal_cdf).astype(jnp.bfloat16)
            grad_pre_ref[pl.ds(base, lane_rows), cols] = (
                grad_act * (normal_cdf + pre_act * density)
            ).astype(jnp.bfloat16)

    def place_rows():
        width = d_width // 8

        @pl.loop(0, 8)
        def _(tile):
            cols = pl.ds(pl.multiple_of(tile * width, 128), width)
            for lane_at in range(place_ref.shape[0]):
                placed = jnp.dot(
                    place_ref[lane_at],
                    packed_all[lane_at, :, cols],
                    preferred_element_type=jnp.float32,
                ).astype(jnp.bfloat16)
                for owner in range(seq_count):
                    routed_all[owner, lane_at * rows : (lane_at + 1) * rows, cols] = placed[
                        owner * rows : (owner + 1) * rows
                    ]

    def partial_rows(lane_at):
        return partial.at[pl.ds(pl.multiple_of(lane_at * rows, 16), rows)]

    def sum_copy(index):
        source, target, lane_to = (
            (partial_rows(sibling), from_sibling.at[0], sibling),
            (partial_rows(diagonal), from_sibling.at[1], sibling),
            (to_across, from_across, across),
        )[index]
        return pltpu.make_async_remote_copy(
            src_ref=source,
            dst_ref=target,
            send_sem=sum_send.at[index],
            recv_sem=sum_recv.at[index],
            device_id=(grp, me, lane_to),
            device_id_type=MESH,
        )

    def own_partial():
        own_pre = pl.ds(pl.multiple_of(me * lane_rows, 16), lane_rows)
        width = m_width // 9

        @pl.loop(0, 9)
        def _(tile):
            cols = pl.ds(pl.multiple_of(tile * width, 128), width)
            partial[:, cols] = dot_nt(grad_pre_ref[own_pre, :], hidden_w[cols, :]).astype(
                jnp.bfloat16
            )

    def unit_and_scale():
        values = features_ref[...].astype(jnp.float32)
        centered = values - jnp.mean(values, axis=1, keepdims=True)
        variance = jnp.mean(centered * centered, axis=1, keepdims=True)
        inv_std = lax.rsqrt(variance + EPSILON)
        return centered * inv_std, inv_std

    own_out(1)
    along_seq(1)
    unit_rows, inv_std = unit_and_scale()
    normed_all[me, pl.ds(pl.multiple_of(lane * rows, 16), rows), :] = (
        unit_rows * gain_ref[...]
    ).astype(jnp.bfloat16)
    own_out(0)
    seq_stage(1, 1)
    along_seq(0)
    across_stage(1, 0)
    seq_stage(1, 2)
    seq_stage(1, 3)
    across_stage(0, 0)
    across_stage(1, 1)
    seq_stage(0, 1)
    sibling_stage(1, 0)
    sibling_stage(0, 0)
    across_stage(1, 2)
    sibling_stage(1, 1)
    seq_stage(0, 2)
    across_stage(1, 3)

    @pl.when(jnp.logical_not(at_end))
    def _():
        seq_stage(0, 3)

    sibling_stage(1, 2)
    sibling_stage(1, 3)
    place_rows()
    across_stage(0, 1)
    load_hidden.wait()
    load_output.wait()
    activate(me)
    own_partial()
    sum_copy(0).start()
    sum_copy(1).start()

    @pl.when(at_end)
    def _():
        seq_stage(0, 3)

    across_stage(0, 2)
    sibling_stage(0, 1)
    activate(plane_at(1))
    sum_copy(1).wait_recv()
    to_across[...] = (
        partial_rows(across)[...].astype(jnp.float32) + from_sibling[1].astype(jnp.float32)
    ).astype(jnp.bfloat16)
    sum_copy(2).start()
    sibling_stage(0, 2)
    activate(plane_at(2))
    d_cut = routed_cut_ref.shape[1]
    for owner in range(seq_count):
        routed_cut_ref[owner * lane_rows : (owner + 1) * lane_rows, :] = routed_all[
            owner, :, pl.ds(pl.multiple_of(me * d_cut, 128), d_cut)
        ]
    across_stage(0, 3)
    sibling_stage(0, 3)
    activate(plane_at(3))
    m_cut = normed_cut_ref.shape[1]
    for owner in range(seq_count):
        normed_cut_ref[owner * lane_rows : (owner + 1) * lane_rows, :] = normed_all[
            owner, :, pl.ds(pl.multiple_of(me * m_cut, 128), m_cut)
        ]
    sum_copy(0).wait_recv()
    sum_copy(2).wait_recv()
    own_grad = (
        partial_rows(lane)[...].astype(jnp.float32)
        + from_sibling[0].astype(jnp.float32)
        + from_across[...].astype(jnp.float32)
    )
    unit_rows, inv_std = unit_and_scale()
    scaled = own_grad * gain_ref[...]
    grad_mean = jnp.mean(scaled, axis=1, keepdims=True)
    cross_mean = jnp.mean(scaled * unit_rows, axis=1, keepdims=True)
    feat_grad_ref[...] = ((scaled - grad_mean - unit_rows * cross_mean) * inv_std).astype(
        jnp.bfloat16
    )

    for index in range(3):
        sum_copy(index).wait_send()
    for kind in (0, 1):
        when_spared(lambda: copy(kind, me, across, PAIR).wait_send())

        @pl.when(has_up)
        def _():
            copy(kind, me, lane, UP).wait_send()

        @pl.when(has_down)
        def _():
            copy(kind, me, lane, DOWN).wait_send()

        for step in range(seq_count):
            plane = plane_at(step)
            if step:
                @pl.when((plane < me) & has_up)
                def _():
                    copy(kind, plane, lane, UP).wait_send()

                @pl.when((plane > me) & has_down)
                def _():
                    copy(kind, plane, lane, DOWN).wait_send()

            when_crossed(step, lambda: copy(kind, plane, lane, ACROSS).wait_send())
            copy(kind, plane, lane, SIBLING).wait_send()
            copy(kind, plane, across, RELAY).wait_send()


def exchange(features, norm_gain, chosen, grad_res, place, hidden_proj, output_proj, seq_count):
    rows, m_width = features.shape
    d_width = grad_res.shape[1]
    h_width = hidden_proj.shape[1]
    lane_count = place.shape[0]
    lane_rows = rows * lane_count
    all_rows = lane_rows * seq_count
    vmem = pl.BlockSpec(memory_space=pltpu.VMEM)
    anywhere = pl.BlockSpec(memory_space=pl.ANY)
    shape = jax.ShapeDtypeStruct
    half = jnp.bfloat16
    return pl.pallas_call(
        exchange_kernel,
        out_shape=(
            shape((all_rows, h_width), half),
            shape((all_rows, h_width), half),
            shape((all_rows, m_width // seq_count), half),
            shape((all_rows, d_width // seq_count), half),
            shape((rows, m_width), half),
        ),
        in_specs=[vmem, vmem, vmem, vmem, vmem, anywhere, anywhere],
        out_specs=(vmem,) * 5,
        scratch_shapes=[
            pltpu.VMEM((m_width, h_width), half),
            pltpu.VMEM((h_width, d_width), half),
            pltpu.VMEM((seq_count, lane_rows, m_width), half),
            pltpu.VMEM((lane_count, seq_count * rows, d_width), half),
            pltpu.VMEM((seq_count, lane_rows, d_width), half),
            pltpu.VMEM((lane_rows, m_width), half),
            pltpu.VMEM((2, rows, m_width), half),
            pltpu.VMEM((rows, m_width), half),
            pltpu.VMEM((rows, m_width), half),
            pltpu.SemaphoreType.DMA((2,)),
            pltpu.SemaphoreType.DMA((2, 6, seq_count)),
            pltpu.SemaphoreType.DMA((2, seq_count, lane_count)),
            pltpu.SemaphoreType.DMA((3,)),
            pltpu.SemaphoreType.DMA((3,)),
        ],
        compiler_params=pltpu.CompilerParams(
            collective_id=0, has_side_effects=True, vmem_limit_bytes=60 * 1024 * 1024
        ),
        cost_estimate=pl.CostEstimate(
            flops=2 * all_rows * h_width * (m_width + d_width),
            bytes_accessed=2 * h_width * (m_width + d_width),
            transcendentals=2 * all_rows * h_width,
        ),
    )(features, norm_gain.reshape(1, m_width), chosen, grad_res, place, hidden_proj, output_proj)


def per_device_gathered(
    grad_res, features, norm_gain, hidden_proj, output_proj, item_start, item_len, item_owner
):
    seq_count = lax.axis_size("seq")
    lane_count = lax.axis_size("tp")
    seq_index = lax.axis_index("seq")
    lane_index = lax.axis_index("tp")
    tok_rows = grad_res.shape[0]
    own_rows = features.shape[0]
    item_count = item_len.shape[1] // lane_count
    first_item = lane_index * item_count
    starts = lax.dynamic_slice(item_start, (seq_index, first_item), (1, item_count))[0]
    lengths = lax.dynamic_slice(item_len, (seq_index, first_item), (1, item_count))[0]
    chosen = chosen_rows(starts, lengths, lane_index * tok_rows, tok_rows, own_rows)
    target = destinations(item_len, item_owner, seq_count, lane_count, own_rows)
    place = jnp.arange(seq_count * own_rows)[None, :, None] == target[:, None, :]
    grad_pre, activated, normed_cut, routed_cut, feat_grad = exchange(
        features,
        norm_gain,
        chosen,
        grad_res,
        place.astype(jnp.bfloat16),
        hidden_proj,
        output_proj,
        seq_count,
    )
    inverse = 1.0 / seq_count
    grad_hidden = (
        jnp.einsum("rm,rh->mh", normed_cut, grad_pre, preferred_element_type=jnp.float32) * inverse
    )
    grad_output = (
        jnp.einsum("rd,rh->dh", routed_cut, activated, preferred_element_type=jnp.float32) * inverse
    )
    return (feat_grad, grad_hidden, grad_output)


def solution(mesh):
    body = per_device_gathered if (mesh.shape["seq"], mesh.shape["tp"]) == (4, 4) else per_device
    in_specs = (
        P(("grp", "seq", "tp"), None),
        P(("grp", "seq", "tp"), None),
        P(),
        P(None, "tp"),
        P("tp", None),
        P("grp", None),
        P("grp", None),
        P("grp", None),
    )
    out_specs = (P(("grp", "seq", "tp"), None), P(("grp", "seq"), "tp"), P(("grp", "seq"), "tp"))
    return jax.shard_map(
        body, mesh=mesh, in_specs=in_specs, out_specs=out_specs, check_vma=False
    )
```
